32 devices in a mesh: tok: 4 (over z), blk: 8 (over y, x, core).
Axes of the slice: x: 2, y: 2, z: 4, core: 2. Of those that a mesh axis runs over, the one named last changes fastest.
Arguments:
- student_in: bfloat16 [7168, 8192], P('tok', 'blk'), may hold values from -6 to 6
- teacher_out: bfloat16 [7168, 8192], P('tok', 'blk'), may hold values from -6 to 6
- w_first: bfloat16 [64, 128, 512], P('blk'), may hold values from -0.5 to 0.5
- w_second: bfloat16 [256, 128, 128], P('blk'), may hold values from -0.5 to 0.5
- w_third: bfloat16 [256, 128, 32], P('blk'), may hold values from -0.5 to 0.5
- w_fourth: bfloat16 [32, 256, 256], P('blk'), may hold values from -0.375 to 0.375
Outputs:
- grad_first: float32 [64, 128, 512], P('blk')
- grad_second: float32 [256, 128, 128], P('blk')
- grad_third: float32 [256, 128, 32], P('blk')
- grad_fourth: float32 [32, 256, 256], P('blk')
The draws below stay inside these ranges and needn't reach their ends.
All inputs are finite; a program needn't handle non-finite values.
Results may differ from the reference program's by a relative error of at most 0.004.
Values may be sent and summed in bfloat16 or wider, within the bound.
No kernel may reach another device: no remote copies, remote signals or barrier semaphores. Data moves between devices by JAX's collectives and lax.ppermute only.
A program may use at most 256 MiB of HBM per device.

```python
import jax
import jax.numpy as jnp
from jax import lax

D = 8192
BW = 128
TOK_DEV = 1792
NA = 64
XS = 2
R = 512
NG = 256
NE = 32
OW = 256
TOKENS = 7168
N_TOK = 4


def block_levels(rng, dims, shards, smallest, top_value):
    level = 1.0
    for dim, blocks in shards:
        steps = jax.random.uniform(jax.random.fold_in(jax.random.fold_in(rng, 6), dim), (blocks,), jnp.float32, smallest / len(shards), top_value / len(shards))
        level = level * jnp.repeat(jnp.exp(steps), dims[dim] // blocks).reshape((-1,) + (1,) * (len(dims) - 1 - dim))
    return level


def scatter_about(stream_key, extent, scale, bound, split=(), dtype=jnp.bfloat16):
    drawn = scale * jax.random.normal(stream_key, extent, jnp.float32)
    if split:
        drawn = drawn * block_levels(stream_key, extent, split, -0.22, 0.18)
    return jnp.clip(drawn, -bound, bound).astype(dtype)


def setup_inputs(seed: int = 0) -> dict:
    seeds = jax.random.split(jax.random.key(seed), 7)
    student_in = scatter_about(seeds[0], (TOKENS, D), 1.0, 6.0, ((0, 4), (1, 8)))
    teacher_out = scatter_about(seeds[1], (TOKENS, D), 1.0, 6.0, ((0, 4), (1, 8)))
    w_first = scatter_about(seeds[2], (NA, BW, R), BW ** -0.5, 0.5, ((0, 8),))
    w_second = scatter_about(seeds[3], (NG, BW, BW), BW ** -0.5, 0.5, ((0, 8),))
    w_third = scatter_about(seeds[4], (NG, BW, NE), BW ** -0.5, 0.5, ((0, 8),))
    w_fourth = scatter_about(seeds[5], (NE, NG, OW), NG ** -0.5, 0.375, ((0, 8),))
    return dict(student_in=student_in, teacher_out=teacher_out, w_first=w_first, w_second=w_second, w_third=w_third, w_fourth=w_fourth)


def gelu_slope(value):
    cdf_part = 0.5 * (1.0 + jax.scipy.special.erf(value * 0.7071067811865476))
    return cdf_part + value * jnp.exp(-0.5 * value * value) * 0.3989422804014327


def reference(student_in, teacher_out, w_first, w_second, w_third, w_fourth):
    f32 = jnp.float32
    bf16 = jnp.bfloat16
    factor = 1.0 / float(TOKENS) ** 0.5
    first_w = w_first.astype(f32)
    second_w = w_second.astype(f32).reshape(NG, NA, XS, BW)
    third_w = w_third.astype(f32)
    fourth_w = w_fourth.astype(f32)
    in_blocks = student_in.reshape(N_TOK, TOK_DEV, NA, BW)
    teach_blocks = teacher_out.reshape(N_TOK, TOK_DEV, NE, OW)

    def step(carry, item):
        acc_first, acc_second, acc_third, acc_fourth = carry
        rows_in, rows_teach = item
        rows_f = rows_in.astype(f32)
        first_out = jnp.einsum("tai,air->tar", rows_f, first_w).astype(bf16).astype(f32)
        first_view = first_out.reshape(TOK_DEV, NA, XS, NG)
        pre_act = jnp.einsum("taxg,gaxo->tgo", first_view, second_w)
        hidden = jax.nn.gelu(pre_act, approximate=False).astype(bf16).astype(f32)
        third_out = jnp.einsum("tgo,goe->tge", hidden, third_w).astype(bf16).astype(f32)
        student = jnp.einsum("tge,ego->teo", third_out, fourth_w)
        slope_out = ((student - rows_teach.astype(f32)) * factor).astype(bf16).astype(f32)
        grad_four = jnp.einsum("tge,teo->ego", third_out, slope_out)
        back_third = jnp.einsum("teo,ego->tge", slope_out, fourth_w).astype(bf16).astype(f32)
        grad_three = jnp.einsum("tgo,tge->goe", hidden, back_third)
        back_hidden = jnp.einsum("tge,goe->tgo", back_third, third_w)
        slope_pre = (back_hidden * gelu_slope(pre_act)).astype(bf16).astype(f32)
        grad_two = jnp.einsum("taxg,tgo->gaxo", first_view, slope_pre).reshape(NG, BW, BW)
        slope_first = jnp.einsum("tgo,gaxo->taxg", slope_pre, second_w).astype(bf16).astype(f32)
        grad_one = jnp.einsum("tai,tar->air", rows_f, slope_first.reshape(TOK_DEV, NA, R))
        return (acc_first + grad_one, acc_second + grad_two, acc_third + grad_three, acc_fourth + grad_four), None

    start = (jnp.zeros((NA, BW, R), f32), jnp.zeros((NG, BW, BW), f32),
             jnp.zeros((NG, BW, NE), f32), jnp.zeros((NE, NG, OW), f32))
    totals, unused = lax.scan(step, start, (in_blocks, teach_blocks))
    return (totals[0], totals[1], totals[2], totals[3])
```

```python
import functools

import jax
import jax.numpy as jnp
from jax import lax
from jax.experimental import pallas as pl
from jax.experimental.pallas import tpu as pltpu
from jax.sharding import PartitionSpec as P

F32 = jnp.float32
BF16 = jnp.bfloat16
TILE = 256
CUTS = (0, 3, 7)
PLAN = ("f0", "f1", "m0", "m1", "q0", "b0", "q1", "b1", "q2", "r0", "x0", "q3", "r1", "x1", "r2", "q4")
ROWS = 16
SUB = 8
LANES = 128
SQRT_HALF = 0.7071067811865476
INV_SQRT_2PI = 0.3989422804014327
VMEM_BYTES = 56 * 1024 * 1024


def nn(a, b):
    return jnp.dot(a, b, preferred_element_type=F32)


def nt(a, b):
    return lax.dot_general(a, b, (((1,), (1,)), ((), ())), preferred_element_type=F32)


def whole(shape):
    return pl.BlockSpec(shape, lambda t: (0,) * len(shape), pipeline_mode=pl.Buffered(1))


def tokens_last(shape):
    lead = len(shape) - 1
    return pl.BlockSpec(shape[:-1] + (TILE,), lambda t: (0,) * lead + (t,))


def piece_spec(shape, row):
    return pl.BlockSpec((TILE, shape[1]), lambda t: (t + row // TILE, 0))


def smem():
    return pl.BlockSpec(memory_space=pltpu.SMEM)


def call(body, grid, in_specs, out_specs, out_shape, scratch, flops, moved):
    return pl.pallas_call(
        body,
        grid=(grid,),
        in_specs=in_specs,
        out_specs=out_specs,
        out_shape=out_shape,
        scratch_shapes=scratch,
        compiler_params=pltpu.CompilerParams(vmem_limit_bytes=VMEM_BYTES),
        cost_estimate=pl.CostEstimate(flops=flops, bytes_accessed=moved, transcendentals=0),
    )


def forward(pieces, order, span, w1, w2_t, w3_t, n_dev):
    n_piece, rows1, in_width = w1.shape
    tok = span[1] - span[0]
    depth1 = pieces[0].shape[1]
    n_a = depth1 // in_width
    n_g, bw, fan = w2_t.shape
    spread = fan // n_piece // n_a
    n_q, third_rows, third_depth = w3_t.shape
    gq = n_g // n_q

    def body(*refs):
        x_refs = refs[:n_piece]
        order_ref, w1_ref, w2_ref, w3_ref, first_ref, third_ref, wide_ref, hid_ref = refs[n_piece:]

        @pl.when(pl.program_id(0) == 0)
        def _():
            owner = lax.broadcasted_iota(jnp.int32, (rows1, in_width), 0) // spread % n_a

            @pl.loop(0, n_piece)
            def _(p):
                rows = w1_ref[p].astype(F32)
                for a in range(n_a):
                    block = jnp.where(owner == a, rows, 0.0).astype(BF16)
                    wide_ref[p, :, a * in_width : (a + 1) * in_width] = block

        for k in range(0, n_piece, 2):
            both = []
            for j in range(2):
                part = nt(wide_ref[order_ref[k + j]], x_refs[k + j][...])
                both.append(part.reshape(n_g, SUB, TILE))
            at = pl.multiple_of(order_ref[k] * SUB, ROWS)
            first_ref[:, pl.ds(at, ROWS), :] = jnp.concatenate(both, axis=1).astype(BF16)

        @pl.loop(0, n_q, unroll=n_q)
        def _(q):
            for j in range(gq):
                pre = nn(w2_ref[q * gq + j], first_ref[q * gq + j])
                cdf = 0.5 * (1.0 + lax.erf(pre * SQRT_HALF))
                hid_ref[j * bw : (j + 1) * bw, :] = (pre * cdf).astype(BF16)
            out = nn(w3_ref[q], hid_ref[...]).astype(BF16)
            third_ref[:, pl.ds(q * ROWS, ROWS), :] = out.reshape(n_dev, ROWS, TILE)

    first_shape = (n_g, fan, tok)
    third_shape = (n_dev, n_q * ROWS, tok)
    return call(
        body,
        tok // TILE,
        [piece_spec(p.shape, span[0]) for p in pieces]
        + [smem(), whole(w1.shape), whole(w2_t.shape), whole(w3_t.shape)],
        [tokens_last(first_shape), tokens_last(third_shape)],
        [jax.ShapeDtypeStruct(first_shape, BF16), jax.ShapeDtypeStruct(third_shape, BF16)],
        [pltpu.VMEM((n_piece, rows1, depth1), BF16), pltpu.VMEM((gq * bw, TILE), BF16)],
        2 * tok * (n_piece * rows1 * depth1 + n_g * bw * fan + n_q * third_rows * third_depth),
        2 * (n_piece * depth1 * tok + w1.size + n_g * fan * tok),
    )(*pieces, order, w1, w2_t, w3_t)


def middle(third, teacher, row, w4_big, w4_big_t, factor, last_local, held_sum, last):
    n_dev, dev_rows, tok = third.shape
    rows, cols = w4_big.shape
    width = cols // last_local
    per_e = rows // last_local
    n_col = width // LANES
    sum_shape = (n_col, rows, LANES)
    grad_shape = (last_local, per_e, width) if last else sum_shape
    sums = [] if held_sum is None else [held_sum]

    def body(third_ref, teach_ref, w4_ref, w4t_ref, *refs):
        start_refs, (back_ref, grad_ref, acc_ref) = refs[: len(sums)], refs[len(sums) :]
        t = pl.program_id(0)

        @pl.when(t == 0)
        def _():
            acc_ref[...] = start_refs[0][...] if sums else jnp.zeros_like(acc_ref)

        held = third_ref[...].reshape(rows, TILE)
        student = nn(w4t_ref[...], held)
        target = teach_ref[...].astype(F32).T
        slope = ((student - target) * factor).astype(BF16)
        back = nn(w4_ref[...], slope).astype(BF16)
        back_ref[...] = back.reshape(n_dev, dev_rows, TILE)
        owner = lax.broadcasted_iota(jnp.int32, (rows, LANES), 0) % last_local
        for e in range(last_local):
            part = nt(held, slope[e * width : (e + 1) * width, :])
            for c in range(n_col):
                cols_c = part[:, c * LANES : (c + 1) * LANES]
                acc_ref[c] += jnp.where(owner == e, cols_c, 0.0)

        @pl.when(t == pl.num_programs(0) - 1)
        def _():
            if not last:
                grad_ref[...] = acc_ref[...]
                return
            for e in range(last_local):
                for c in range(n_col):
                    picked = acc_ref[c, pl.ds(e, per_e, stride=last_local), :]
                    grad_ref[e, :, c * LANES : (c + 1) * LANES] = picked

    return call(
        body,
        tok // TILE,
        [
            tokens_last(third.shape),
            pl.BlockSpec((TILE, cols), lambda t: (t + row // TILE, 0)),
            whole(w4_big.shape),
            whole(w4_big_t.shape),
        ]
        + [whole(a.shape) for a in sums],
        [tokens_last(third.shape), whole(grad_shape)],
        [jax.ShapeDtypeStruct(third.shape, BF16), jax.ShapeDtypeStruct(grad_shape, F32)],
        [pltpu.VMEM(sum_shape, F32)],
        6 * tok * rows * cols,
        2 * (3 * third.size + 2 * rows * cols),
    )(third, teacher, w4_big, w4_big_t, *sums)


def backward(turns, first, back, w2, w2_t, w3, sums, last):
    n_dev = back.shape[0]
    n_g, fan, tok = first.shape
    bw = w2.shape[2]
    n_q = w3.shape[0]
    gq = n_g // n_q
    last_local = ROWS // gq
    n_e = n_dev * last_local
    sum_shapes = [(n_g, fan, bw), (n_q, gq * bw, n_dev * ROWS)]
    out_shapes = [(n_g, fan + n_e, bw)] if last else sum_shapes
    n_out = len(out_shapes)

    def body(*refs):
        (turn_ref, first_ref, back_ref, w2_ref, w2t_ref, w3_ref), refs = refs[:6], refs[6:]
        start_refs, refs = refs[: len(sums)], refs[len(sums) :]
        slope_ref, *out_refs = refs[: n_out + 1]
        hid_ref, *acc_refs = refs[n_out + 1 :]
        acc_refs = acc_refs if last else out_refs
        acc2_ref, acc3_ref = acc_refs
        t = pl.program_id(0)

        @pl.when(t == 0)
        def _():
            for i in range(2):
                start = start_refs[i][...] if sums else jnp.zeros_like(acc_refs[i])
                acc_refs[i][...] = start

        @pl.loop(0, n_q, unroll=n_q)
        def _(q):
            held = back_ref[:, pl.ds(q * ROWS, ROWS), :].reshape(n_dev * ROWS, TILE)
            both, slopes = [], []
            for j in range(gq):
                g = q * gq + j
                pre = nn(w2t_ref[g], first_ref[g])
                cdf = 0.5 * (1.0 + lax.erf(pre * SQRT_HALF))
                hid_ref[j * bw : (j + 1) * bw, :] = (pre * cdf).astype(BF16)
                rise = cdf + pre * jnp.exp(-0.5 * pre * pre) * INV_SQRT_2PI
                back_hidden = nn(w3_ref[q, j * bw : (j + 1) * bw, :], held)
                slope = (back_hidden * rise).astype(BF16)
                slopes.append(slope)
                both.append(nn(w2_ref[g], slope).reshape(fan // SUB, SUB, TILE))
                if j % 2:
                    left = first_ref[pl.ds(g - 1, 2)].reshape(2 * fan, TILE)
                    prod = nt(left, jnp.concatenate(slopes, axis=0))
                    acc2_ref[g - 1] += prod[:fan, :bw]
                    acc2_ref[g] += prod[fan:, bw:]
                    at = pl.multiple_of((g - 1) * SUB, ROWS)
                    pair = jnp.concatenate(both, axis=1).astype(BF16)
                    slope_ref[:, pl.ds(at, ROWS), :] = pair
                    both, slopes = [], []
            acc3_ref[q] += nt(hid_ref[...], held)

        @pl.when(t == pl.num_programs(0) - 1 if last else False)
        def _():
            turn_g = turn_ref[1]
            col = lax.broadcasted_iota(jnp.int32, (n_e, n_dev * ROWS), 1)
            entry = lax.broadcasted_iota(jnp.int32, (n_e, n_dev * ROWS), 0)
            pick = (col // ROWS * last_local + col % last_local == entry).astype(F32)
            lane = lax.broadcasted_iota(jnp.int32, (bw, n_dev * ROWS), 1) % ROWS // last_local

            @pl.loop(0, n_q)
            def _(q):
                for j in range(gq):
                    g = q * gq + j
                    to = g ^ turn_g
                    out_refs[0][to, :fan, :] = acc2_ref[g]
                    rows = jnp.where(lane == j, acc3_ref[q, j * bw : (j + 1) * bw, :], 0.0)
                    out_refs[0][to, fan:, :] = lax.dot_general(
                        pick,
                        rows,
                        (((1,), (1,)), ((), ())),
                        precision=lax.Precision.HIGHEST,
                        preferred_element_type=F32,
                    )

    slope_shape = (fan // SUB, n_g * SUB, tok)
    return call(
        body,
        tok // TILE,
        [smem(), tokens_last(first.shape), tokens_last(back.shape)]
        + [whole(a.shape) for a in (w2, w2_t, w3, *sums)],
        [tokens_last(slope_shape)] + [whole(shape) for shape in out_shapes],
        [jax.ShapeDtypeStruct(slope_shape, BF16)]
        + [jax.ShapeDtypeStruct(shape, F32) for shape in out_shapes],
        [pltpu.VMEM((gq * bw, TILE), BF16)]
        + [pltpu.VMEM(shape, F32) for shape in sum_shapes if last],
        2 * tok * 6 * n_g * bw * fan,
        2 * (2 * first.size + back.size),
    )(turns, first, back, w2, w2_t, w3, *sums)


def first_grad(pieces, order, row, turns, slope, n_g, in_width, held_sum, last):
    n_piece, rows, tok = slope.shape
    depth1 = pieces[0].shape[1]
    n_a = depth1 // in_width
    spread = SUB // n_a
    sums = [] if held_sum is None else [held_sum]
    sum_shape = (n_piece, rows, in_width)
    out_shape = (2 * n_a, n_piece // 2, spread, n_g, in_width) if last else sum_shape

    def body(*refs):
        x_refs, refs = refs[:n_piece], refs[n_piece:]
        (order_ref, turn_ref, slope_ref), refs = refs[:3], refs[3:]
        start_refs, out_ref = refs[: len(sums)], refs[len(sums)]
        acc_ref = refs[-1]
        t = pl.program_id(0)

        @pl.when(t == 0)
        def _():
            acc_ref[...] = start_refs[0][...] if sums else jnp.zeros_like(acc_ref)

        owner = lax.broadcasted_iota(jnp.int32, (rows, in_width), 0) // spread % n_a
        for k in range(n_piece):
            p = order_ref[k]
            prod = nn(slope_ref[p], x_refs[k][...])
            total = acc_ref[p]
            for a in range(n_a):
                total += jnp.where(owner == a, prod[:, a * in_width : (a + 1) * in_width], 0.0)
            acc_ref[p] = total

        @pl.when(t == pl.num_programs(0) - 1 if last else False)
        def _():
            turn_a = turn_ref[0]
            for p in range(n_piece):
                for r in range(SUB):
                    a = p % 2 * n_a + r // spread
                    picked = acc_ref[p, pl.ds(r, n_g, stride=SUB), :]
                    out_ref[a ^ turn_a, p // 2, r % spread] = picked

    return call(
        body,
        tok // TILE,
        [piece_spec(p.shape, row) for p in pieces]
        + [smem(), smem(), tokens_last(slope.shape)]
        + [whole(a.shape) for a in sums],
        whole(out_shape),
        jax.ShapeDtypeStruct(out_shape, F32),
        [pltpu.VMEM(sum_shape, F32)] if last else [],
        2 * tok * n_piece * rows * depth1,
        2 * (n_piece * depth1 * tok + slope.size),
    )(*pieces, order, turns, slope, *sums)


def rows_to_out(rows_by_part):
    return jnp.concatenate([r.astype(F32) for r in rows_by_part], axis=0).T


def unpack_first(parts, spread):
    n_dev, local, _, n_g, in_width = parts.shape

    def body(in_ref, out_ref):
        out_ref[0] = rows_to_out([in_ref[d, 0, x] for x in range(spread) for d in range(n_dev)])

    out_cols = spread * n_dev * n_g
    return pl.pallas_call(
        body,
        grid=(local,),
        in_specs=[pl.BlockSpec((n_dev, 1, spread, n_g, in_width), lambda a: (0, a, 0, 0, 0))],
        out_specs=pl.BlockSpec((1, in_width, out_cols), lambda a: (a, 0, 0)),
        out_shape=jax.ShapeDtypeStruct((local, in_width, out_cols), F32),
        compiler_params=pltpu.CompilerParams(vmem_limit_bytes=VMEM_BYTES),
    )(parts)


def in_vmem():
    return pl.BlockSpec(memory_space=pltpu.VMEM)


def unpack_ring_first(halves, me, spread):
    n_dev, _, n_g, in_width = halves[0][0].shape
    local = 2 * len(halves[0])

    def body(me_ref, *refs):
        ins, out_ref = refs[:-1], refs[-1]
        for h in range(2):
            for k in range(local // 2):
                piece = ins[h * (local // 2) + k]
                rows = [piece[d, x] for x in range(spread) for d in range(n_dev)]
                out_ref[(me_ref[0] ^ k) * 2 + h] = rows_to_out(rows)

    return pl.pallas_call(
        body,
        in_specs=[smem()] + [in_vmem()] * local,
        out_specs=in_vmem(),
        out_shape=jax.ShapeDtypeStruct((local, in_width, spread * n_dev * n_g), F32),
        compiler_params=pltpu.CompilerParams(vmem_limit_bytes=VMEM_BYTES),
    )(me, *halves[0], *halves[1])


def unpack_ring_rest(halves, me, fan):
    some, rows, bw = halves[0][0].shape
    n_own = len(halves[0])
    n_g = 2 * n_own * some

    def body(me_ref, *refs):
        ins, (g2_ref, g3_ref) = refs[:-2], refs[-2:]
        for h in range(2):
            for k in range(n_own):
                piece = ins[h * n_own + k]
                base = ((me_ref[0] ^ k) * 2 + h) * some
                for j in range(some):
                    g2_ref[base + j] = piece[j, :fan, :].astype(F32)
                    g3_ref[base + j] = piece[j, fan:, :].astype(F32)

    return pl.pallas_call(
        body,
        in_specs=[smem()] + [in_vmem()] * (2 * n_own),
        out_specs=[in_vmem(), in_vmem()],
        out_shape=[
            jax.ShapeDtypeStruct((n_g, fan, bw), F32),
            jax.ShapeDtypeStruct((n_g, rows - fan, bw), F32),
        ],
        compiler_params=pltpu.CompilerParams(vmem_limit_bytes=VMEM_BYTES),
    )(me, *halves[0], *halves[1])


def swap(x):
    return lax.all_to_all(x, "blk", split_axis=0, concat_axis=0, tiled=True)


def turn(x, axis, bits):
    n = lax.axis_size(axis)
    return lax.ppermute(x, axis, [(i, i ^ bits) for i in range(n)])


def follow(x, *before):
    return lax.optimization_barrier((x, before))[0]


SIDES = ((1, 3), (3, 1))


def ring_send(parts, near):
    return turn(jnp.stack([parts[near], parts[2]]).astype(BF16), "tok", near)


def ring_half(parts, got, far):
    mine = parts[0] + got[0].astype(F32)
    theirs = parts[far] + got[1].astype(F32)
    return mine, turn(theirs.astype(BF16), "tok", far)


def ring_scatter(parts, near, far):
    mine, got = ring_half(parts, ring_send(parts, near), far)
    return mine + got.astype(F32)


def ring_gather(mine, near, far):
    other = turn(mine, "tok", far)
    got = turn(jnp.stack([mine, other]), "tok", near)
    parts = {0: mine, far: other, near: got[0], 2: got[1]}
    return [parts[k] for k in range(4)]


def gather_pieces(x, hold):
    half = x.shape[1] // 2
    low, high = x[:, :half], x[:, half:]
    one = [turn(p, "blk", 2) for p in (low, high)]
    two = [turn(p, "blk", 4) for p in (low, high)]
    one, two = follow((one, two), hold)
    both = [turn(one[0], "blk", 4), turn(two[1], "blk", 2)]
    pieces = []
    for group in ((low, high), one, two, both):
        pieces.extend(group)
        pieces.extend(turn(p, "blk", 1) for p in group)
    return pieces


def shards(cuts, student_in, teacher_out, w_first, w_second, w_third, w_fourth):
    n_dev = lax.axis_size("blk")
    n_tok = lax.axis_size("tok")
    tok_rows = student_in.shape[0]
    first_local, in_width, first_cols = w_first.shape
    n_first = first_local * n_dev
    n_g, fan, bw = w_second.shape
    n_second = n_g * n_dev
    spread = first_cols // n_second
    last_local, _, out_width = w_fourth.shape
    factor = 1.0 / float(tok_rows * n_tok) ** 0.5
    n_a = SUB // spread
    n_piece = n_first // n_a
    gq = ROWS // last_local
    n_q = n_g // gq
    me_tok = lax.axis_index("tok").astype(jnp.int32)
    ring = n_tok == 4 and first_local == 8 and n_g % 8 == 0
    turns = jnp.array([2, n_g // 4], jnp.int32) * (me_tok if ring else 0)

    n_chunks = len(cuts) - 1
    bounds = [(tok_rows * lo // cuts[-1], tok_rows * hi // cuts[-1]) for lo, hi in zip(cuts, cuts[1:])]

    cols = w_first.reshape(first_local, in_width, spread, n_dev, n_g).transpose(3, 0, 2, 4, 1)
    cols = swap(cols)
    w2_t = w_second.transpose(0, 2, 1)
    same_g = jnp.eye(gq, dtype=BF16)[None, :, None, None, :, None]
    w3_big = w_third.reshape(n_q, gq, bw, n_dev, 1, last_local) * same_g
    w3_big = w3_big.reshape(n_q, gq * bw, n_dev * ROWS)
    w3_t = w3_big.transpose(0, 2, 1)
    same_e = jnp.eye(last_local, dtype=BF16)[None, :, :, None]
    w4_big = (w_fourth.transpose(1, 0, 2)[:, :, None, :] * same_e).reshape(
        n_second * last_local, last_local * out_width
    )
    w4_t = w4_big.T
    w3_t, w4_big, w4_t = [follow(w, cols) for w in (w3_t, w4_big, w4_t)]
    w1 = cols.reshape(n_piece, n_a, spread, n_g, in_width).transpose(0, 3, 1, 2, 4)
    w1 = w1.reshape(n_piece, n_g * SUB, in_width)
    w1 = follow(w1, w3_t, w4_big, w4_t)

    order = jnp.arange(n_piece, dtype=jnp.int32)
    if n_dev == 8 and first_local == 2 * n_a:
        order = order ^ (2 * lax.axis_index("blk")).astype(jnp.int32)
        pieces = gather_pieces(student_in, (w1, w3_big, w3_t, w4_big, w4_t))
    else:
        x_all = lax.all_gather(student_in, "blk", axis=0)
        pieces = [p for d in range(n_dev) for p in jnp.split(x_all[d], n_piece // n_dev, axis=1)]

    firsts, thirds, backs, slopes, own_rest = [], [], [], [], []
    sums = ()
    grad_four = part_one = None
    done = ()

    def do_forward(c):
        nonlocal done
        first, third = forward(pieces, follow(order, done), bounds[c], w1, w2_t, w3_t, n_dev)
        firsts.append(first)
        thirds.append(swap(third))
        done = third

    def do_middle(c):
        nonlocal done, grad_four
        back, grad_four = middle(
            follow(thirds[c], done), teacher_out, bounds[c][0], w4_big, w4_t, factor, last_local,
            grad_four, c == n_chunks - 1,
        )
        backs.append(swap(back))
        done = back

    def do_backward(c):
        nonlocal done, sums
        slope, *sums = backward(
            follow(turns, done), firsts[c], backs[c], w_second, w2_t, w3_big, sums, c == n_chunks - 1
        )
        slopes.append(slope)
        done = slope

    def do_first_grad(c):
        nonlocal done, part_one, grad_four
        last = c == n_chunks - 1
        part_one = first_grad(
            pieces, order, bounds[c][0], follow(turns, done), slopes[c], n_g, in_width, part_one, last
        )
        done = part_one

    ring_state = {}

    def do_ring(c):
        nonlocal done
        if not ring:
            return
        if c == 0:
            rest = sums[0].reshape(4, 2, n_g // 8, *sums[0].shape[1:])
            ring_state["parts"] = [rest[:, h] for h in range(2)]
            ring_state["got"] = [ring_send(rest[:, h], SIDES[h][0]) for h in range(2)]
            return
        got = follow(ring_state["got"], done)
        if c == 1:
            halves = [ring_half(ring_state["parts"][h], got[h], SIDES[h][1]) for h in range(2)]
            ring_state["mine"], ring_state["got"] = zip(*halves)
            done = (done, ring_state["mine"])
            return
        pairs = zip(ring_state["mine"], got)
        own_rest.extend((mine + part.astype(F32)).astype(BF16) for mine, part in pairs)

    four = {}

    def do_ring_four(c):
        nonlocal done, grad_four
        if not ring:
            return
        near, far = SIDES[0]
        rank = me_tok ^ jnp.arange(4)
        if c == 0:
            four["shape"] = grad_four.shape
            parts = jnp.take(grad_four.reshape(4, -1, LANES), rank, axis=0)
            four["parts"], four["got"] = parts, ring_send(parts, near)
        elif c == 1:
            got = follow(four["got"], done)
            four["mine"], four["got"] = ring_half(four["parts"], got, far)
            done = (done, four["mine"])
        elif c == 2:
            got = follow(four["got"], done)
            four["own"] = (four["mine"] + got.astype(F32)).astype(BF16)
            four["other"] = turn(four["own"], "tok", far)
            done = (done, four["own"])
        elif c == 3:
            pair = jnp.stack([four["own"], follow(four["other"], done)])
            four["pair"], four["got"] = pair, turn(pair, "tok", near)
            done = (done, pair)
        else:
            pair, got = four["pair"], follow(four["got"], done)
            parts = {0: pair[0], far: pair[1], near: got[0], 2: got[1]}
            parts = jnp.stack([parts[k] for k in range(4)])
            grad_four = jnp.take(parts, rank, axis=0).reshape(four["shape"]).astype(F32)

    steps = {
        "q": do_ring_four,
        "r": do_ring,
        "f": do_forward,
        "m": do_middle,
        "b": do_backward,
        "x": do_first_grad,
    }
    for step in PLAN:
        steps[step[0]](int(step[1]))
    rest = sums[0]
    if not ring:
        grad_four, rest = lax.psum((grad_four.astype(BF16), rest.astype(BF16)), "tok")
        grad_two, grad_three = rest[:, :fan].astype(F32), rest[:, fan:].astype(F32)
        part_one = part_one.transpose(1, 0, 2, 3, 4)
        part_one = part_one.reshape(n_dev, first_local, spread, n_g, in_width).astype(BF16)
        grad_one = unpack_first(lax.psum(swap(part_one), "tok"), spread)
        return (grad_one, grad_two, grad_three.transpose(0, 2, 1), grad_four.astype(F32))

    me = me_tok.reshape(1)
    rest_halves = [ring_gather(own_rest[h], *SIDES[h]) for h in range(2)]
    grad_two, grad_three = unpack_ring_rest(rest_halves, me, fan)
    one = part_one.reshape(4, 2, n_dev, spread, n_g, in_width)
    own = [ring_scatter(one[:, h], *SIDES[h]).astype(BF16) for h in range(2)]
    own = swap(jnp.stack(own, axis=1))
    one_halves = [ring_gather(own[:, h], *SIDES[h]) for h in range(2)]
    grad_one = unpack_ring_first(one_halves, me, spread)
    return (grad_one, grad_two, grad_three.transpose(0, 2, 1), grad_four)


def solution(mesh):
    placed = (
        P("tok", "blk"),
        P("tok", "blk"),
        P("blk", None, None),
        P("blk", None, None),
        P("blk", None, None),
        P("blk", None, None),
    )
    return jax.shard_map(
        functools.partial(shards, CUTS),
        mesh=mesh,
        in_specs=placed,
        out_specs=(
            P("blk", None, None),
            P("blk", None, None),
            P("blk", None, None),
            P("blk", None, None),
        ),
        check_vma=False,
    )
```

```python
import functools

import jax
import jax.numpy as jnp
from jax import lax
from jax.experimental import pallas as pl
from jax.experimental.pallas import tpu as pltpu
from jax.sharding import PartitionSpec as P

F32 = jnp.float32
BF16 = jnp.bfloat16
TILE = 256
CUTS = (0, 3, 7)
PLAN = ("g0", "h0", "f0", "g1", "m0", "h1", "f1", "s0", "m1", "q0", "d0", "q1", "x0", "s1", "q2", "x1", "q3", "r0", "d1", "q4", "r1")
ROWS = 16
SUB = 8
LANES = 128
SQRT_HALF = 0.7071067811865476
INV_SQRT_2PI = 0.3989422804014327
VMEM_BYTES = 56 * 1024 * 1024


def nn(a, b):
    return jnp.dot(a, b, preferred_element_type=F32)


def nt(a, b):
    return lax.dot_general(a, b, (((1,), (1,)), ((), ())), preferred_element_type=F32)


def whole(shape):
    return pl.BlockSpec(shape, lambda t: (0,) * len(shape), pipeline_mode=pl.Buffered(1))


def tokens_last(shape):
    lead = len(shape) - 1
    return pl.BlockSpec(shape[:-1] + (TILE,), lambda t: (0,) * lead + (t,))


def piece_spec(shape):
    return pl.BlockSpec((TILE, shape[1]), lambda t: (t, 0))


def smem():
    return pl.BlockSpec(memory_space=pltpu.SMEM)


def call(body, grid, in_specs, out_specs, out_shape, scratch, flops, moved):
    return pl.pallas_call(
        body,
        grid=(grid,),
        in_specs=in_specs,
        out_specs=out_specs,
        out_shape=out_shape,
        scratch_shapes=scratch,
        compiler_params=pltpu.CompilerParams(vmem_limit_bytes=VMEM_BYTES),
        cost_estimate=pl.CostEstimate(flops=flops, bytes_accessed=moved, transcendentals=0),
    )


def forward(pieces, order, w1, w2_t, w3_t, n_dev):
    n_piece, rows1, in_width = w1.shape
    tok = pieces[0].shape[0]
    depth1 = pieces[0].shape[1]
    n_a = depth1 // in_width
    n_g, bw, fan = w2_t.shape
    spread = fan // n_piece // n_a
    n_q, third_rows, third_depth = w3_t.shape
    gq = n_g // n_q

    def body(*refs):
        x_refs = refs[:n_piece]
        order_ref, w1_ref, w2_ref, w3_ref, first_ref, third_ref, wide_ref, hid_ref = refs[n_piece:]

        @pl.when(pl.program_id(0) == 0)
        def _():
            owner = lax.broadcasted_iota(jnp.int32, (rows1, in_width), 0) // spread % n_a

            @pl.loop(0, n_piece)
            def _(p):
                rows = w1_ref[p].astype(F32)
                for a in range(n_a):
                    block = jnp.where(owner == a, rows, 0.0).astype(BF16)
                    wide_ref[p, :, a * in_width : (a + 1) * in_width] = block

        for k in range(0, n_piece, 2):
            both = []
            for j in range(2):
                part = nt(wide_ref[order_ref[k + j]], x_refs[k + j][...])
                both.append(part.reshape(n_g, SUB, TILE))
            at = pl.multiple_of(order_ref[k] * SUB, ROWS)
            first_ref[:, pl.ds(at, ROWS), :] = jnp.concatenate(both, axis=1).astype(BF16)

        @pl.loop(0, n_q, unroll=n_q)
        def _(q):
            for j in range(gq):
                pre = nn(w2_ref[q * gq + j], first_ref[q * gq + j])
                cdf = 0.5 * (1.0 + lax.erf(pre * SQRT_HALF))
                hid_ref[j * bw : (j + 1) * bw, :] = (pre * cdf).astype(BF16)
            out = nn(w3_ref[q], hid_ref[...]).astype(BF16)
            third_ref[:, pl.ds(q * ROWS, ROWS), :] = out.reshape(n_dev, ROWS, TILE)

    first_shape = (n_g, fan, tok)
    third_shape = (n_dev, n_q * ROWS, tok)
    return call(
        body,
        tok // TILE,
        [piece_spec(p.shape) for p in pieces]
        + [smem(), whole(w1.shape), whole(w2_t.shape), whole(w3_t.shape)],
        [tokens_last(first_shape), tokens_last(third_shape)],
        [jax.ShapeDtypeStruct(first_shape, BF16), jax.ShapeDtypeStruct(third_shape, BF16)],
        [pltpu.VMEM((n_piece, rows1, depth1), BF16), pltpu.VMEM((gq * bw, TILE), BF16)],
        2 * tok * (n_piece * rows1 * depth1 + n_g * bw * fan + n_q * third_rows * third_depth),
        2 * (n_piece * depth1 * tok + w1.size + n_g * fan * tok),
    )(*pieces, order, w1, w2_t, w3_t)


def middle(third, teacher, row, w4_big, w4_big_t, factor, last_local, held_sum, last):
    n_dev, dev_rows, tok = third.shape
    rows, cols = w4_big.shape
    width = cols // last_local
    per_e = rows // last_local
    n_col = width // LANES
    sum_shape = (n_col, rows, LANES)
    grad_shape = (last_local, per_e, width) if last else sum_shape
    sums = [] if held_sum is None else [held_sum]

    def body(third_ref, teach_ref, w4_ref, w4t_ref, *refs):
        start_refs, (back_ref, grad_ref, acc_ref) = refs[: len(sums)], refs[len(sums) :]
        t = pl.program_id(0)

        @pl.when(t == 0)
        def _():
            acc_ref[...] = start_refs[0][...] if sums else jnp.zeros_like(acc_ref)

        held = third_ref[...].reshape(rows, TILE)
        student = nn(w4t_ref[...], held)
        target = teach_ref[...].astype(F32).T
        slope = ((student - target) * factor).astype(BF16)
        back = nn(w4_ref[...], slope).astype(BF16)
        back_ref[...] = back.reshape(n_dev, dev_rows, TILE)
        owner = lax.broadcasted_iota(jnp.int32, (rows, LANES), 0) % last_local
        for e in range(last_local):
            part = nt(held, slope[e * width : (e + 1) * width, :])
            for c in range(n_col):
                cols_c = part[:, c * LANES : (c + 1) * LANES]
                acc_ref[c] += jnp.where(owner == e, cols_c, 0.0)

        @pl.when(t == pl.num_programs(0) - 1)
        def _():
            if not last:
                grad_ref[...] = acc_ref[...]
                return
            for e in range(last_local):
                for c in range(n_col):
                    picked = acc_ref[c, pl.ds(e, per_e, stride=last_local), :]
                    grad_ref[e, :, c * LANES : (c + 1) * LANES] = picked

    return call(
        body,
        tok // TILE,
        [
            tokens_last(third.shape),
            pl.BlockSpec((TILE, cols), lambda t: (t + row // TILE, 0)),
            whole(w4_big.shape),
            whole(w4_big_t.shape),
        ]
        + [whole(a.shape) for a in sums],
        [tokens_last(third.shape), whole(grad_shape)],
        [jax.ShapeDtypeStruct(third.shape, BF16), jax.ShapeDtypeStruct(grad_shape, F32)],
        [pltpu.VMEM(sum_shape, F32)],
        6 * tok * rows * cols,
        2 * (3 * third.size + 2 * rows * cols),
    )(third, teacher, w4_big, w4_big_t, *sums)


def slopes_back(order, first, back, w2, w2_t, w3):
    n_dev = back.shape[0]
    n_g, fan, tok = first.shape
    bw = w2.shape[2]
    n_q = w3.shape[0]
    gq = n_g // n_q

    def body(order_ref, first_ref, back_ref, w2_ref, w2t_ref, w3_ref, slope_ref, pre_ref, hid_ref):
        @pl.loop(0, n_q, unroll=n_q)
        def _(q):
            held = back_ref[:, pl.ds(q * ROWS, ROWS), :].reshape(n_dev * ROWS, TILE)
            both = []
            for j in range(gq):
                g = q * gq + j
                pre = nn(w2t_ref[g], first_ref[g])
                cdf = 0.5 * (1.0 + lax.erf(pre * SQRT_HALF))
                hid_ref[q, j * bw : (j + 1) * bw, :] = (pre * cdf).astype(BF16)
                rise = cdf + pre * jnp.exp(-0.5 * pre * pre) * INV_SQRT_2PI
                back_hidden = nn(w3_ref[q, j * bw : (j + 1) * bw, :], held)
                slope = (back_hidden * rise).astype(BF16)
                pre_ref[g] = slope
                both.append(nn(w2_ref[g], slope).reshape(fan // SUB, SUB, TILE))
                if j % 2:
                    at = pl.multiple_of((g - 1) * SUB, ROWS)
                    pair = jnp.concatenate(both, axis=1).astype(BF16)
                    slope_ref[:, pl.ds(at, ROWS), :] = pair
                    both = []

    shapes = [(fan // SUB, n_g * SUB, tok), (n_g, bw, tok), (n_q, gq * bw, tok)]
    return call(
        body,
        tok // TILE,
        [smem(), tokens_last(first.shape), tokens_last(back.shape)]
        + [whole(a.shape) for a in (w2, w2_t, w3)],
        [tokens_last(shape) for shape in shapes],
        [jax.ShapeDtypeStruct(shape, BF16) for shape in shapes],
        [],
        2 * tok * 4 * n_g * bw * fan,
        2 * (4 * first.size + back.size),
    )(order, first, back, w2, w2_t, w3)


def second_grads(turns, first, slope, hidden, back, sums, last):
    n_dev = back.shape[0]
    n_g, fan, tok = first.shape
    bw = slope.shape[1]
    n_q = hidden.shape[0]
    gq = n_g // n_q
    last_local = ROWS // gq
    n_e = n_dev * last_local
    sum_shapes = [(n_g, fan, bw), (n_q, gq * bw, n_dev * ROWS)]
    out_shapes = [(n_g, fan + n_e, bw)] if last else sum_shapes
    n_out = len(out_shapes)

    def body(turn_ref, first_ref, slope_ref, hid_ref, back_ref, *refs):
        start_refs, refs = refs[: len(sums)], refs[len(sums) :]
        out_refs, acc_refs = refs[:n_out], refs[n_out:]
        acc_refs = acc_refs if last else out_refs
        acc2_ref, acc3_ref = acc_refs
        t = pl.program_id(0)

        @pl.when(t == 0)
        def _():
            for i in range(2):
                start = start_refs[i][...] if sums else jnp.zeros_like(acc_refs[i])
                acc_refs[i][...] = start

        @pl.loop(0, n_q, unroll=n_q)
        def _(q):
            held = back_ref[:, pl.ds(q * ROWS, ROWS), :].reshape(n_dev * ROWS, TILE)
            for j in range(0, gq, 2):
                g = q * gq + j
                left = first_ref[pl.ds(g, 2)].reshape(2 * fan, TILE)
                prod = nt(left, slope_ref[pl.ds(g, 2)].reshape(2 * bw, TILE))
                acc2_ref[g] += prod[:fan, :bw]
                acc2_ref[g + 1] += prod[fan:, bw:]
            acc3_ref[q] += nt(hid_ref[q], held)

        @pl.when(t == pl.num_programs(0) - 1 if last else False)
        def _():
            turn_g = turn_ref[1]
            col = lax.broadcasted_iota(jnp.int32, (n_e, n_dev * ROWS), 1)
            entry = lax.broadcasted_iota(jnp.int32, (n_e, n_dev * ROWS), 0)
            pick = (col // ROWS * last_local + col % last_local == entry).astype(F32)
            lane = lax.broadcasted_iota(jnp.int32, (bw, n_dev * ROWS), 1) % ROWS // last_local

            @pl.loop(0, n_q)
            def _(q):
                for j in range(gq):
                    g = q * gq + j
                    to = g ^ turn_g
                    out_refs[0][to, :fan, :] = acc2_ref[g]
                    rows = jnp.where(lane == j, acc3_ref[q, j * bw : (j + 1) * bw, :], 0.0)
                    out_refs[0][to, fan:, :] = lax.dot_general(
                        pick,
                        rows,
                        (((1,), (1,)), ((), ())),
                        precision=lax.Precision.HIGHEST,
                        preferred_element_type=F32,
                    )

    return call(
        body,
        tok // TILE,
        [smem()]
        + [tokens_last(a.shape) for a in (first, slope, hidden, back)]
        + [whole(a.shape) for a in sums],
        [whole(shape) for shape in out_shapes],
        [jax.ShapeDtypeStruct(shape, F32) for shape in out_shapes],
        [pltpu.VMEM(shape, F32) for shape in sum_shapes if last],
        2 * tok * 2 * n_g * bw * fan,
        2 * (3 * first.size + back.size),
    )(turns, first, slope, hidden, back, *sums)


def first_grad(pieces, order, turns, slope, n_g, in_width, held_sum, last):
    n_piece, rows, tok = slope.shape
    depth1 = pieces[0].shape[1]
    n_a = depth1 // in_width
    spread = SUB // n_a
    sums = [] if held_sum is None else [held_sum]
    sum_shape = (n_piece, rows, in_width)
    out_shape = (2 * n_a, n_piece // 2, spread, n_g, in_width) if last else sum_shape

    def body(*refs):
        x_refs, refs = refs[:n_piece], refs[n_piece:]
        (order_ref, turn_ref, slope_ref), refs = refs[:3], refs[3:]
        start_refs, out_ref = refs[: len(sums)], refs[len(sums)]
        acc_ref = refs[-1]
        t = pl.program_id(0)

        @pl.when(t == 0)
        def _():
            acc_ref[...] = start_refs[0][...] if sums else jnp.zeros_like(acc_ref)

        owner = lax.broadcasted_iota(jnp.int32, (rows, in_width), 0) // spread % n_a
        for k in range(n_piece):
            p = order_ref[k]
            prod = nn(slope_ref[p], x_refs[k][...])
            total = acc_ref[p]
            for a in range(n_a):
                total += jnp.where(owner == a, prod[:, a * in_width : (a + 1) * in_width], 0.0)
            acc_ref[p] = total

        @pl.when(t == pl.num_programs(0) - 1 if last else False)
        def _():
            turn_a = turn_ref[0]
            for p in range(n_piece):
                for r in range(SUB):
                    a = p % 2 * n_a + r // spread
                    picked = acc_ref[p, pl.ds(r, n_g, stride=SUB), :]
                    out_ref[a ^ turn_a, p // 2, r % spread] = picked

    return call(
        body,
        tok // TILE,
        [piece_spec(p.shape) for p in pieces]
        + [smem(), smem(), tokens_last(slope.shape)]
        + [whole(a.shape) for a in sums],
        whole(out_shape),
        jax.ShapeDtypeStruct(out_shape, F32),
        [pltpu.VMEM(sum_shape, F32)] if last else [],
        2 * tok * n_piece * rows * depth1,
        2 * (n_piece * depth1 * tok + slope.size),
    )(*pieces, order, turns, slope, *sums)


def rows_to_out(rows_by_part):
    return jnp.concatenate([r.astype(F32) for r in rows_by_part], axis=0).T


def unpack_first(parts, spread):
    n_dev, local, _, n_g, in_width = parts.shape

    def body(in_ref, out_ref):
        out_ref[0] = rows_to_out([in_ref[d, 0, x] for x in range(spread) for d in range(n_dev)])

    out_cols = spread * n_dev * n_g
    return pl.pallas_call(
        body,
        grid=(local,),
        in_specs=[pl.BlockSpec((n_dev, 1, spread, n_g, in_width), lambda a: (0, a, 0, 0, 0))],
        out_specs=pl.BlockSpec((1, in_width, out_cols), lambda a: (a, 0, 0)),
        out_shape=jax.ShapeDtypeStruct((local, in_width, out_cols), F32),
        compiler_params=pltpu.CompilerParams(vmem_limit_bytes=VMEM_BYTES),
    )(parts)


def in_vmem():
    return pl.BlockSpec(memory_space=pltpu.VMEM)


def unpack_ring_first(halves, me, spread):
    n_dev, _, n_g, in_width = halves[0][0].shape
    local = 2 * len(halves[0])

    def body(me_ref, *refs):
        ins, out_ref = refs[:-1], refs[-1]
        for h in range(2):
            for k in range(local // 2):
                piece = ins[h * (local // 2) + k]
                rows = [piece[d, x] for x in range(spread) for d in range(n_dev)]
                out_ref[(me_ref[0] ^ k) * 2 + h] = rows_to_out(rows)

    return pl.pallas_call(
        body,
        in_specs=[smem()] + [in_vmem()] * local,
        out_specs=in_vmem(),
        out_shape=jax.ShapeDtypeStruct((local, in_width, spread * n_dev * n_g), F32),
        compiler_params=pltpu.CompilerParams(vmem_limit_bytes=VMEM_BYTES),
    )(me, *halves[0], *halves[1])


def unpack_ring_rest(halves, me, fan):
    some, rows, bw = halves[0][0].shape
    n_own = len(halves[0])
    n_g = 2 * n_own * some

    def body(me_ref, *refs):
        ins, (g2_ref, g3_ref) = refs[:-2], refs[-2:]
        for h in range(2):
            for k in range(n_own):
                piece = ins[h * n_own + k]
                base = ((me_ref[0] ^ k) * 2 + h) * some
                for j in range(some):
                    g2_ref[base + j] = piece[j, :fan, :].astype(F32)
                    g3_ref[base + j] = piece[j, fan:, :].astype(F32)

    return pl.pallas_call(
        body,
        in_specs=[smem()] + [in_vmem()] * (2 * n_own),
        out_specs=[in_vmem(), in_vmem()],
        out_shape=[
            jax.ShapeDtypeStruct((n_g, fan, bw), F32),
            jax.ShapeDtypeStruct((n_g, rows - fan, bw), F32),
        ],
        compiler_params=pltpu.CompilerParams(vmem_limit_bytes=VMEM_BYTES),
    )(me, *halves[0], *halves[1])


def swap(x):
    return lax.all_to_all(x, "blk", split_axis=0, concat_axis=0, tiled=True)


def turn(x, axis, bits):
    n = lax.axis_size(axis)
    return lax.ppermute(x, axis, [(i, i ^ bits) for i in range(n)])


def follow(x, *before):
    return lax.optimization_barrier((x, before))[0]


SIDES = ((1, 3), (3, 1))


def ring_send(parts, near):
    return turn(jnp.stack([parts[near], parts[2]]).astype(BF16), "tok", near)


def ring_half(parts, got, far):
    mine = parts[0] + got[0].astype(F32)
    theirs = parts[far] + got[1].astype(F32)
    return mine, turn(theirs.astype(BF16), "tok", far)


def ring_scatter(parts, near, far):
    mine, got = ring_half(parts, ring_send(parts, near), far)
    return mine + got.astype(F32)


def ring_gather(mine, near, far):
    other = turn(mine, "tok", far)
    got = turn(jnp.stack([mine, other]), "tok", near)
    parts = {0: mine, far: other, near: got[0], 2: got[1]}
    return [parts[k] for k in range(4)]


def gather_pieces(x, before, hold):
    x = follow(x, before)
    half = x.shape[1] // 2
    low, high = x[:, :half], x[:, half:]
    one = [turn(p, "blk", 2) for p in (low, high)]
    two = [turn(p, "blk", 4) for p in (low, high)]
    near = [turn(p, "blk", 1) for p in (low, high)]
    one, two = follow((one, two), near, hold)
    both = [turn(one[0], "blk", 4), turn(two[1], "blk", 2)]
    pieces = [low, high] + near
    for group in (one, two):
        pieces.extend(group)
        pieces.extend(turn(p, "blk", 1) for p in group)
    return pieces + both


def shards(cuts, student_in, teacher_out, w_first, w_second, w_third, w_fourth):
    n_dev = lax.axis_size("blk")
    n_tok = lax.axis_size("tok")
    tok_rows = student_in.shape[0]
    first_local, in_width, first_cols = w_first.shape
    n_first = first_local * n_dev
    n_g, fan, bw = w_second.shape
    n_second = n_g * n_dev
    spread = first_cols // n_second
    last_local, _, out_width = w_fourth.shape
    factor = 1.0 / float(tok_rows * n_tok) ** 0.5
    n_a = SUB // spread
    n_piece = n_first // n_a
    gq = ROWS // last_local
    n_q = n_g // gq
    me_tok = lax.axis_index("tok").astype(jnp.int32)
    ring = n_tok == 4 and first_local == 8 and n_g % 8 == 0
    turns = jnp.array([2, n_g // 4], jnp.int32) * (me_tok if ring else 0)

    n_chunks = len(cuts) - 1
    bounds = [(tok_rows * lo // cuts[-1], tok_rows * hi // cuts[-1]) for lo, hi in zip(cuts, cuts[1:])]

    cols = w_first.reshape(first_local, in_width, spread, n_dev, n_g).transpose(3, 0, 2, 4, 1)
    cols = swap(cols)
    w2_t = w_second.transpose(0, 2, 1)
    same_g = jnp.eye(gq, dtype=BF16)[None, :, None, None, :, None]
    w3_big = w_third.reshape(n_q, gq, bw, n_dev, 1, last_local) * same_g
    w3_big = w3_big.reshape(n_q, gq * bw, n_dev * ROWS)
    w3_t = w3_big.transpose(0, 2, 1)
    same_e = jnp.eye(last_local, dtype=BF16)[None, :, :, None]
    w4_big = (w_fourth.transpose(1, 0, 2)[:, :, None, :] * same_e).reshape(
        n_second * last_local, last_local * out_width
    )
    w4_t = w4_big.T
    w3_t, w4_big, w4_t = [follow(w, cols) for w in (w3_t, w4_big, w4_t)]
    w1 = cols.reshape(n_piece, n_a, spread, n_g, in_width).transpose(0, 3, 1, 2, 4)
    w1 = w1.reshape(n_piece, n_g * SUB, in_width)
    w1 = follow(w1, w3_t, w4_big, w4_t)

    order = jnp.arange(n_piece, dtype=jnp.int32)
    paired = n_dev == 8 and first_local == 2 * n_a
    if paired:
        order = order ^ (2 * lax.axis_index("blk")).astype(jnp.int32)
    gathered = []
    prepared = (w1, w3_big, w3_t, w4_big, w4_t)

    def do_gather(c):
        x = student_in[bounds[c][0] : bounds[c][1]]
        if paired:
            gathered.append(gather_pieces(x, gathered[-1:], done if c else prepared))
            return
        x_all = lax.all_gather(x, "blk", axis=0)
        each = n_piece // n_dev
        gathered.append([p for d in range(n_dev) for p in jnp.split(x_all[d], each, axis=1)])

    firsts, thirds, backs, slopes = [], [], [], []
    sums = ()
    grad_four = part_one = None
    done = ()

    def do_last_pieces(c):
        if paired:
            both = follow(gathered[c][-2:], done)
            gathered[c] = gathered[c][:-2] + both + [turn(p, "blk", 1) for p in both]

    def do_forward(c):
        nonlocal done
        first, third = forward(gathered[c], follow(order, done), w1, w2_t, w3_t, n_dev)
        firsts.append(first)
        thirds.append(swap(third))
        done = third

    def do_middle(c):
        nonlocal done, grad_four
        back, grad_four = middle(
            follow(thirds[c], done), teacher_out, bounds[c][0], w4_big, w4_t, factor, last_local,
            grad_four, c == n_chunks - 1,
        )
        backs.append(swap(back))
        done = back

    def do_slopes(c):
        nonlocal done
        slope, *kept = slopes_back(
            follow(order, done), firsts[c], backs[c], w_second, w2_t, w3_big
        )
        slopes.append((slope, *kept))
        done = slope

    def do_second_grads(c):
        nonlocal done, sums
        _, *kept = slopes[c]
        sums = second_grads(
            follow(turns, done), firsts[c], *kept, backs[c], sums, c == n_chunks - 1
        )
        done = sums

    def do_first_grad(c):
        nonlocal done, part_one, grad_four
        last = c == n_chunks - 1
        part_one = first_grad(
            gathered[c], order, follow(turns, done), slopes[c][0], n_g, in_width, part_one, last
        )
        done = part_one

    one_state = {}

    def do_ring_one(c):
        if not ring:
            return
        if c == 0:
            one = part_one.reshape(4, 2, n_dev, spread, n_g, in_width)
            one_state["parts"] = [one[:, h] for h in range(2)]
            one_state["got"] = [ring_send(one[:, h], SIDES[h][0]) for h in range(2)]
            return
        got = follow(one_state["got"], done)
        one_state["own"] = []
        for h in range(2):
            mine, part = ring_half(one_state["parts"][h], got[h], SIDES[h][1])
            one_state["own"].append((mine + part.astype(F32)).astype(BF16))

    four = {}

    def do_ring_four(c):
        nonlocal done, grad_four
        if not ring:
            return
        near, far = SIDES[0]
        rank = me_tok ^ jnp.arange(4)
        if c == 0:
            four["shape"] = grad_four.shape
            parts = jnp.take(grad_four.reshape(4, -1, LANES), rank, axis=0)
            four["parts"], four["got"] = parts, ring_send(parts, near)
        elif c == 1:
            got = follow(four["got"], done)
            four["mine"], four["got"] = ring_half(four["parts"], got, far)
            done = (done, four["mine"])
        elif c == 2:
            got = follow(four["got"], done)
            four["own"] = (four["mine"] + got.astype(F32)).astype(BF16)
            four["other"] = turn(four["own"], "tok", far)
            done = (done, four["own"])
        elif c == 3:
            pair = jnp.stack([four["own"], follow(four["other"], done)])
            four["pair"], four["got"] = pair, turn(pair, "tok", near)
            done = (done, pair)
        else:
            pair, got = four["pair"], follow(four["got"], done)
            parts = {0: pair[0], far: pair[1], near: got[0], 2: got[1]}
            parts = jnp.stack([parts[k] for k in range(4)])
            grad_four = jnp.take(parts, rank, axis=0).reshape(four["shape"]).astype(F32)

    steps = {
        "g": do_gather,
        "h": do_last_pieces,
        "q": do_ring_four,
        "r": do_ring_one,
        "f": do_forward,
        "m": do_middle,
        "s": do_slopes,
        "d": do_second_grads,
        "x": do_first_grad,
    }
    for step in PLAN:
        steps[step[0]](int(step[1]))
    rest = sums[0]
    if not ring:
        grad_four, rest = lax.psum((grad_four.astype(BF16), rest.astype(BF16)), "tok")
        grad_two, grad_three = rest[:, :fan].astype(F32), rest[:, fan:].astype(F32)
        part_one = part_one.transpose(1, 0, 2, 3, 4)
        part_one = part_one.reshape(n_dev, first_local, spread, n_g, in_width).astype(BF16)
        grad_one = unpack_first(lax.psum(swap(part_one), "tok"), spread)
        return (grad_one, grad_two, grad_three.transpose(0, 2, 1), grad_four.astype(F32))

    me = me_tok.reshape(1)
    own = swap(jnp.stack(one_state["own"], axis=1))
    rest = rest.reshape(4, 2, n_g // 8, *rest.shape[1:])
    rest_halves = []
    for h in range(2):
        mine = ring_scatter(rest[:, h], *SIDES[h]).astype(BF16)
        rest_halves.append(ring_gather(mine, *SIDES[h]))
    grad_two, grad_three = unpack_ring_rest(rest_halves, me, fan)
    one_halves = [ring_gather(own[:, h], *SIDES[h]) for h in range(2)]
    grad_one = unpack_ring_first(one_halves, me, spread)
    return (grad_one, grad_two, grad_three.transpose(0, 2, 1), grad_four)


def solution(mesh):
    placed = (
        P("tok", "blk"),
        P("tok", "blk"),
        P("blk", None, None),
        P("blk", None, None),
        P("blk", None, None),
        P("blk", None, None),
    )
    return jax.shard_map(
        functools.partial(shards, CUTS),
        mesh=mesh,
        in_specs=placed,
        out_specs=(
            P("blk", None, None),
            P("blk", None, None),
            P("blk", None, None),
            P("blk", None, None),
        ),
        check_vma=False,
    )
```

```python
import functools

import jax
import jax.numpy as jnp
from jax import lax
from jax.experimental import pallas as pl
from jax.experimental.pallas import tpu as pltpu
from jax.sharding import PartitionSpec as P

F32 = jnp.float32
BF16 = jnp.bfloat16
TILE = 256
CUTS = (0, 3, 7)
PLAN = ("g0", "h0", "f0", "g1", "m0", "h1", "f1", "s0", "m1", "q0", "d0", "q1", "x0", "s1", "q2", "x1", "q3", "r0", "d1", "q4", "r1")
ROWS = 16
SUB = 8
LANES = 128
SQRT_HALF = 0.7071067811865476
INV_SQRT_2PI = 0.3989422804014327
VMEM_BYTES = 56 * 1024 * 1024


def nn(a, b):
    return jnp.dot(a, b, preferred_element_type=F32)


def nt(a, b):
    return lax.dot_general(a, b, (((1,), (1,)), ((), ())), preferred_element_type=F32)


def whole(shape):
    return pl.BlockSpec(shape, lambda t: (0,) * len(shape), pipeline_mode=pl.Buffered(1))


def tokens_last(shape):
    lead = len(shape) - 1
    return pl.BlockSpec(shape[:-1] + (TILE,), lambda t: (0,) * lead + (t,))


def piece_spec(shape):
    return pl.BlockSpec((TILE, shape[1]), lambda t: (t, 0))


def smem():
    return pl.BlockSpec(memory_space=pltpu.SMEM)


def call(body, grid, in_specs, out_specs, out_shape, scratch, flops, moved):
    return pl.pallas_call(
        body,
        grid=(grid,),
        in_specs=in_specs,
        out_specs=out_specs,
        out_shape=out_shape,
        scratch_shapes=scratch,
        compiler_params=pltpu.CompilerParams(vmem_limit_bytes=VMEM_BYTES),
        cost_estimate=pl.CostEstimate(flops=flops, bytes_accessed=moved, transcendentals=0),
    )


def forward(pieces, order, w1, w2_t, w3_t, n_dev):
    n_piece, rows1, in_width = w1.shape
    tok = pieces[0].shape[0]
    depth1 = pieces[0].shape[1]
    n_a = depth1 // in_width
    n_g, bw, fan = w2_t.shape
    spread = fan // n_piece // n_a
    n_q, third_rows, third_depth = w3_t.shape
    gq = n_g // n_q

    def body(*refs):
        x_refs = refs[:n_piece]
        order_ref, w1_ref, w2_ref, w3_ref, first_ref, third_ref, wide_ref, hid_ref = refs[n_piece:]

        @pl.when(pl.program_id(0) == 0)
        def _():
            owner = lax.broadcasted_iota(jnp.int32, (rows1, in_width), 0) // spread % n_a

            @pl.loop(0, n_piece)
            def _(p):
                rows = w1_ref[p].astype(F32)
                for a in range(n_a):
                    block = jnp.where(owner == a, rows, 0.0).astype(BF16)
                    wide_ref[p, :, a * in_width : (a + 1) * in_width] = block

        for k in range(0, n_piece, 2):
            both = []
            for j in range(2):
                part = nt(wide_ref[order_ref[k + j]], x_refs[k + j][...])
                both.append(part.reshape(n_g, SUB, TILE))
            at = pl.multiple_of(order_ref[k] * SUB, ROWS)
            first_ref[:, pl.ds(at, ROWS), :] = jnp.concatenate(both, axis=1).astype(BF16)

        @pl.loop(0, n_q, unroll=n_q)
        def _(q):
            for j in range(gq):
                pre = nn(w2_ref[q * gq + j], first_ref[q * gq + j])
                cdf = 0.5 * (1.0 + lax.erf(pre * SQRT_HALF))
                hid_ref[j * bw : (j + 1) * bw, :] = (pre * cdf).astype(BF16)
            out = nn(w3_ref[q], hid_ref[...]).astype(BF16)
            third_ref[:, pl.ds(q * ROWS, ROWS), :] = out.reshape(n_dev, ROWS, TILE)

    first_shape = (n_g, fan, tok)
    third_shape = (n_dev, n_q * ROWS, tok)
    return call(
        body,
        tok // TILE,
        [piece_spec(p.shape) for p in pieces]
        + [smem(), whole(w1.shape), whole(w2_t.shape), whole(w3_t.shape)],
        [tokens_last(first_shape), tokens_last(third_shape)],
        [jax.ShapeDtypeStruct(first_shape, BF16), jax.ShapeDtypeStruct(third_shape, BF16)],
        [pltpu.VMEM((n_piece, rows1, depth1), BF16), pltpu.VMEM((gq * bw, TILE), BF16)],
        2 * tok * (n_piece * rows1 * depth1 + n_g * bw * fan + n_q * third_rows * third_depth),
        2 * (n_piece * depth1 * tok + w1.size + n_g * fan * tok),
    )(*pieces, order, w1, w2_t, w3_t)


def middle(third, teacher, row, w4_big, w4_big_t, factor, last_local, held_sum, last):
    n_dev, dev_rows, tok = third.shape
    rows, cols = w4_big.shape
    width = cols // last_local
    per_e = rows // last_local
    n_col = width // LANES
    sum_shape = (n_col, rows, LANES)
    grad_shape = (last_local, per_e, width) if last else sum_shape
    sums = [] if held_sum is None else [held_sum]

    def body(third_ref, teach_ref, w4_ref, w4t_ref, *refs):
        start_refs, (back_ref, grad_ref, acc_ref) = refs[: len(sums)], refs[len(sums) :]
        t = pl.program_id(0)

        @pl.when(t == 0)
        def _():
            acc_ref[...] = start_refs[0][...] if sums else jnp.zeros_like(acc_ref)

        held = third_ref[...].reshape(rows, TILE)
        student = nn(w4t_ref[...], held)
        target = teach_ref[...].astype(F32).T
        slope = ((student - target) * factor).astype(BF16)
        back = nn(w4_ref[...], slope).astype(BF16)
        back_ref[...] = back.reshape(n_dev, dev_rows, TILE)
        owner = lax.broadcasted_iota(jnp.int32, (rows, LANES), 0) % last_local
        for e in range(last_local):
            part = nt(held, slope[e * width : (e + 1) * width, :])
            for c in range(n_col):
                cols_c = part[:, c * LANES : (c + 1) * LANES]
                acc_ref[c] += jnp.where(owner == e, cols_c, 0.0)

        @pl.when(t == pl.num_programs(0) - 1)
        def _():
            if not last:
                grad_ref[...] = acc_ref[...]
                return
            for e in range(last_local):
                for c in range(n_col):
                    picked = acc_ref[c, pl.ds(e, per_e, stride=last_local), :]
                    grad_ref[e, :, c * LANES : (c + 1) * LANES] = picked

    return call(
        body,
        tok // TILE,
        [
            tokens_last(third.shape),
            pl.BlockSpec((TILE, cols), lambda t: (t + row // TILE, 0)),
            whole(w4_big.shape),
            whole(w4_big_t.shape),
        ]
        + [whole(a.shape) for a in sums],
        [tokens_last(third.shape), whole(grad_shape)],
        [jax.ShapeDtypeStruct(third.shape, BF16), jax.ShapeDtypeStruct(grad_shape, F32)],
        [pltpu.VMEM(sum_shape, F32)],
        6 * tok * rows * cols,
        2 * (3 * third.size + 2 * rows * cols),
    )(third, teacher, w4_big, w4_big_t, *sums)


def slopes_back(order, first, back, w2, w2_t, w3):
    n_dev = back.shape[0]
    n_g, fan, tok = first.shape
    bw = w2.shape[2]
    n_q = w3.shape[0]
    gq = n_g // n_q

    def body(order_ref, first_ref, back_ref, w2_ref, w2t_ref, w3_ref, slope_ref, pre_ref, hid_ref):
        @pl.loop(0, n_q, unroll=n_q)
        def _(q):
            held = back_ref[:, pl.ds(q * ROWS, ROWS), :].reshape(n_dev * ROWS, TILE)
            both = []
            for j in range(gq):
                g = q * gq + j
                pre = nn(w2t_ref[g], first_ref[g])
                cdf = 0.5 * (1.0 + lax.erf(pre * SQRT_HALF))
                hid_ref[q, j * bw : (j + 1) * bw, :] = (pre * cdf).astype(BF16)
                rise = cdf + pre * jnp.exp(-0.5 * pre * pre) * INV_SQRT_2PI
                back_hidden = nn(w3_ref[q, j * bw : (j + 1) * bw, :], held)
                slope = (back_hidden * rise).astype(BF16)
                pre_ref[g] = slope
                both.append(nn(w2_ref[g], slope).reshape(fan // SUB, SUB, TILE))
                if j % 2:
                    at = pl.multiple_of((g - 1) * SUB, ROWS)
                    pair = jnp.concatenate(both, axis=1).astype(BF16)
                    slope_ref[:, pl.ds(at, ROWS), :] = pair
                    both = []

    shapes = [(fan // SUB, n_g * SUB, tok), (n_g, bw, tok), (n_q, gq * bw, tok)]
    return call(
        body,
        tok // TILE,
        [smem(), tokens_last(first.shape), tokens_last(back.shape)]
        + [whole(a.shape) for a in (w2, w2_t, w3)],
        [tokens_last(shape) for shape in shapes],
        [jax.ShapeDtypeStruct(shape, BF16) for shape in shapes],
        [],
        2 * tok * 4 * n_g * bw * fan,
        2 * (4 * first.size + back.size),
    )(order, first, back, w2, w2_t, w3)


def second_grads(turns, first, slope, hidden, back, sums, last):
    n_dev = back.shape[0]
    n_g, fan, tok = first.shape
    bw = slope.shape[1]
    n_q = hidden.shape[0]
    gq = n_g // n_q
    last_local = ROWS // gq
    n_e = n_dev * last_local
    sum_shapes = [(n_g, fan, bw), (n_q, gq * bw, n_dev * ROWS)]
    out_shapes = [(n_g, fan + n_e, bw)] if last else sum_shapes
    n_out = len(out_shapes)

    def body(turn_ref, first_ref, slope_ref, hid_ref, back_ref, *refs):
        start_refs, refs = refs[: len(sums)], refs[len(sums) :]
        out_refs, acc_refs = refs[:n_out], refs[n_out:]
        acc_refs = acc_refs if last else out_refs
        acc2_ref, acc3_ref = acc_refs
        t = pl.program_id(0)

        @pl.when(t == 0)
        def _():
            for i in range(2):
                start = start_refs[i][...] if sums else jnp.zeros_like(acc_refs[i])
                acc_refs[i][...] = start

        @pl.loop(0, n_q, unroll=n_q)
        def _(q):
            held = back_ref[:, pl.ds(q * ROWS, ROWS), :].reshape(n_dev * ROWS, TILE)
            for j in range(0, gq, 2):
                g = q * gq + j
                left = first_ref[pl.ds(g, 2)].reshape(2 * fan, TILE)
                prod = nt(left, slope_ref[pl.ds(g, 2)].reshape(2 * bw, TILE))
                acc2_ref[g] += prod[:fan, :bw]
                acc2_ref[g + 1] += prod[fan:, bw:]
            acc3_ref[q] += nt(hid_ref[q], held)

        @pl.when(t == pl.num_programs(0) - 1 if last else False)
        def _():
            turn_g = turn_ref[1]
            col = lax.broadcasted_iota(jnp.int32, (n_e, n_dev * ROWS), 1)
            entry = lax.broadcasted_iota(jnp.int32, (n_e, n_dev * ROWS), 0)
            pick = (col // ROWS * last_local + col % last_local == entry).astype(F32)
            lane = lax.broadcasted_iota(jnp.int32, (bw, n_dev * ROWS), 1) % ROWS // last_local

            @pl.loop(0, n_q)
            def _(q):
                for j in range(gq):
                    g = q * gq + j
                    to = g ^ turn_g
                    out_refs[0][to, :fan, :] = acc2_ref[g].astype(BF16)
                    rows = jnp.where(lane == j, acc3_ref[q, j * bw : (j + 1) * bw, :], 0.0)
                    out_refs[0][to, fan:, :] = lax.dot_general(
                        pick,
                        rows,
                        (((1,), (1,)), ((), ())),
                        precision=lax.Precision.HIGHEST,
                        preferred_element_type=F32,
                    ).astype(BF16)

    return call(
        body,
        tok // TILE,
        [smem()]
        + [tokens_last(a.shape) for a in (first, slope, hidden, back)]
        + [whole(a.shape) for a in sums],
        [whole(shape) for shape in out_shapes],
        [jax.ShapeDtypeStruct(shape, BF16 if last else F32) for shape in out_shapes],
        [pltpu.VMEM(shape, F32) for shape in sum_shapes if last],
        2 * tok * 2 * n_g * bw * fan,
        2 * (3 * first.size + back.size),
    )(turns, first, slope, hidden, back, *sums)


def first_grad(pieces, order, turns, slope, n_g, in_width, held_sum, last):
    n_piece, rows, tok = slope.shape
    depth1 = pieces[0].shape[1]
    n_a = depth1 // in_width
    spread = SUB // n_a
    sums = [] if held_sum is None else [held_sum]
    sum_shape = (n_piece, rows, in_width)
    out_shape = (2 * n_a, n_piece // 2, spread, n_g, in_width) if last else sum_shape

    def body(*refs):
        x_refs, refs = refs[:n_piece], refs[n_piece:]
        (order_ref, turn_ref, slope_ref), refs = refs[:3], refs[3:]
        start_refs, out_ref = refs[: len(sums)], refs[len(sums)]
        acc_ref = refs[-1]
        t = pl.program_id(0)

        @pl.when(t == 0)
        def _():
            acc_ref[...] = start_refs[0][...] if sums else jnp.zeros_like(acc_ref)

        owner = lax.broadcasted_iota(jnp.int32, (rows, in_width), 0) // spread % n_a
        for k in range(n_piece):
            p = order_ref[k]
            prod = nn(slope_ref[p], x_refs[k][...])
            total = acc_ref[p]
            for a in range(n_a):
                total += jnp.where(owner == a, prod[:, a * in_width : (a + 1) * in_width], 0.0)
            acc_ref[p] = total

        @pl.when(t == pl.num_programs(0) - 1 if last else False)
        def _():
            turn_a = turn_ref[0]
            for p in range(n_piece):
                for r in range(SUB):
                    a = p % 2 * n_a + r // spread
                    picked = acc_ref[p, pl.ds(r, n_g, stride=SUB), :]
                    out_ref[a ^ turn_a, p // 2, r % spread] = picked.astype(BF16)

    return call(
        body,
        tok // TILE,
        [piece_spec(p.shape) for p in pieces]
        + [smem(), smem(), tokens_last(slope.shape)]
        + [whole(a.shape) for a in sums],
        whole(out_shape),
        jax.ShapeDtypeStruct(out_shape, BF16 if last else F32),
        [pltpu.VMEM(sum_shape, F32)] if last else [],
        2 * tok * n_piece * rows * depth1,
        2 * (n_piece * depth1 * tok + slope.size),
    )(*pieces, order, turns, slope, *sums)


def rows_to_out(rows_by_part):
    return jnp.concatenate([r.astype(F32) for r in rows_by_part], axis=0).T


def unpack_first(parts, spread):
    n_dev, local, _, n_g, in_width = parts.shape

    def body(in_ref, out_ref):
        out_ref[0] = rows_to_out([in_ref[d, 0, x] for x in range(spread) for d in range(n_dev)])

    out_cols = spread * n_dev * n_g
    return pl.pallas_call(
        body,
        grid=(local,),
        in_specs=[pl.BlockSpec((n_dev, 1, spread, n_g, in_width), lambda a: (0, a, 0, 0, 0))],
        out_specs=pl.BlockSpec((1, in_width, out_cols), lambda a: (a, 0, 0)),
        out_shape=jax.ShapeDtypeStruct((local, in_width, out_cols), F32),
        compiler_params=pltpu.CompilerParams(vmem_limit_bytes=VMEM_BYTES),
    )(parts)


def in_vmem():
    return pl.BlockSpec(memory_space=pltpu.VMEM)


def unpack_ring_first(halves, me, spread):
    n_dev, _, n_g, in_width = halves[0][0].shape
    local = 2 * len(halves[0])

    def body(me_ref, *refs):
        ins, out_ref = refs[:-1], refs[-1]
        for h in range(2):
            for k in range(local // 2):
                piece = ins[h * (local // 2) + k]
                rows = [piece[d, x] for x in range(spread) for d in range(n_dev)]
                out_ref[(me_ref[0] ^ k) * 2 + h] = rows_to_out(rows)

    return pl.pallas_call(
        body,
        in_specs=[smem()] + [in_vmem()] * local,
        out_specs=in_vmem(),
        out_shape=jax.ShapeDtypeStruct((local, in_width, spread * n_dev * n_g), F32),
        compiler_params=pltpu.CompilerParams(vmem_limit_bytes=VMEM_BYTES),
    )(me, *halves[0], *halves[1])


def unpack_ring_rest(halves, me, fan):
    some, rows, bw = halves[0][0].shape
    n_own = len(halves[0])
    n_g = 2 * n_own * some

    def body(me_ref, *refs):
        ins, (g2_ref, g3_ref) = refs[:-2], refs[-2:]
        for h in range(2):
            for k in range(n_own):
                piece = ins[h * n_own + k]
                base = ((me_ref[0] ^ k) * 2 + h) * some
                for j in range(some):
                    g2_ref[base + j] = piece[j, :fan, :].astype(F32)
                    g3_ref[base + j] = piece[j, fan:, :].astype(F32)

    return pl.pallas_call(
        body,
        in_specs=[smem()] + [in_vmem()] * (2 * n_own),
        out_specs=[in_vmem(), in_vmem()],
        out_shape=[
            jax.ShapeDtypeStruct((n_g, fan, bw), F32),
            jax.ShapeDtypeStruct((n_g, rows - fan, bw), F32),
        ],
        compiler_params=pltpu.CompilerParams(vmem_limit_bytes=VMEM_BYTES),
    )(me, *halves[0], *halves[1])


def swap(x):
    return lax.all_to_all(x, "blk", split_axis=0, concat_axis=0, tiled=True)


def turn(x, axis, bits):
    n = lax.axis_size(axis)
    return lax.ppermute(x, axis, [(i, i ^ bits) for i in range(n)])


def follow(x, *before):
    return lax.optimization_barrier((x, before))[0]


SIDES = ((1, 3), (3, 1))


def ring_send(parts, near):
    return turn(jnp.stack([parts[near], parts[2]]).astype(BF16), "tok", near)


def ring_half(parts, got, far):
    mine = parts[0] + got[0].astype(F32)
    theirs = parts[far] + got[1].astype(F32)
    return mine, turn(theirs.astype(BF16), "tok", far)


def ring_scatter(parts, near, far):
    mine, got = ring_half(parts, ring_send(parts, near), far)
    return mine + got.astype(F32)


def ring_gather(mine, near, far):
    other = turn(mine, "tok", far)
    got = turn(jnp.stack([mine, other]), "tok", near)
    parts = {0: mine, far: other, near: got[0], 2: got[1]}
    return [parts[k] for k in range(4)]


def gather_pieces(x, before, hold):
    x = follow(x, before)
    half = x.shape[1] // 2
    low, high = x[:, :half], x[:, half:]
    one = [turn(p, "blk", 2) for p in (low, high)]
    two = [turn(p, "blk", 4) for p in (low, high)]
    near = [turn(p, "blk", 1) for p in (low, high)]
    one, two = follow((one, two), near, hold)
    both = [turn(one[0], "blk", 4), turn(two[1], "blk", 2)]
    pieces = [low, high] + near
    for group in (one, two):
        pieces.extend(group)
        pieces.extend(turn(p, "blk", 1) for p in group)
    return pieces + both


def shards(cuts, student_in, teacher_out, w_first, w_second, w_third, w_fourth):
    n_dev = lax.axis_size("blk")
    n_tok = lax.axis_size("tok")
    tok_rows = student_in.shape[0]
    first_local, in_width, first_cols = w_first.shape
    n_first = first_local * n_dev
    n_g, fan, bw = w_second.shape
    n_second = n_g * n_dev
    spread = first_cols // n_second
    last_local, _, out_width = w_fourth.shape
    factor = 1.0 / float(tok_rows * n_tok) ** 0.5
    n_a = SUB // spread
    n_piece = n_first // n_a
    gq = ROWS // last_local
    n_q = n_g // gq
    me_tok = lax.axis_index("tok").astype(jnp.int32)
    ring = n_tok == 4 and first_local == 8 and n_g % 8 == 0
    turns = jnp.array([2, n_g // 4], jnp.int32) * (me_tok if ring else 0)

    n_chunks = len(cuts) - 1
    bounds = [(tok_rows * lo // cuts[-1], tok_rows * hi // cuts[-1]) for lo, hi in zip(cuts, cuts[1:])]

    cols = w_first.reshape(first_local, in_width, spread, n_dev, n_g).transpose(3, 0, 2, 4, 1)
    cols = swap(cols)
    w2_t = w_second.transpose(0, 2, 1)
    same_g = jnp.eye(gq, dtype=BF16)[None, :, None, None, :, None]
    w3_big = w_third.reshape(n_q, gq, bw, n_dev, 1, last_local) * same_g
    w3_big = w3_big.reshape(n_q, gq * bw, n_dev * ROWS)
    w3_t = w3_big.transpose(0, 2, 1)
    same_e = jnp.eye(last_local, dtype=BF16)[None, :, :, None]
    w4_big = (w_fourth.transpose(1, 0, 2)[:, :, None, :] * same_e).reshape(
        n_second * last_local, last_local * out_width
    )
    w4_t = w4_big.T
    w3_t, w4_big, w4_t = [follow(w, cols) for w in (w3_t, w4_big, w4_t)]
    w1 = cols.reshape(n_piece, n_a, spread, n_g, in_width).transpose(0, 3, 1, 2, 4)
    w1 = w1.reshape(n_piece, n_g * SUB, in_width)
    w1 = follow(w1, w3_t, w4_big, w4_t)

    order = jnp.arange(n_piece, dtype=jnp.int32)
    paired = n_dev == 8 and first_local == 2 * n_a
    if paired:
        order = order ^ (2 * lax.axis_index("blk")).astype(jnp.int32)
    gathered = []
    prepared = (w1, w3_big, w3_t, w4_big, w4_t)

    def do_gather(c):
        x = student_in[bounds[c][0] : bounds[c][1]]
        if paired:
            gathered.append(gather_pieces(x, gathered[-1:], done if c else prepared))
            return
        x_all = lax.all_gather(x, "blk", axis=0)
        each = n_piece // n_dev
        gathered.append([p for d in range(n_dev) for p in jnp.split(x_all[d], each, axis=1)])

    firsts, thirds, backs, slopes = [], [], [], []
    sums = ()
    grad_four = part_one = None
    done = ()

    def do_last_pieces(c):
        if paired:
            both = follow(gathered[c][-2:], done)
            gathered[c] = gathered[c][:-2] + both + [turn(p, "blk", 1) for p in both]

    def do_forward(c):
        nonlocal done
        first, third = forward(gathered[c], follow(order, done), w1, w2_t, w3_t, n_dev)
        firsts.append(first)
        thirds.append(swap(third))
        done = third

    def do_middle(c):
        nonlocal done, grad_four
        back, grad_four = middle(
            follow(thirds[c], done), teacher_out, bounds[c][0], w4_big, w4_t, factor, last_local,
            grad_four, c == n_chunks - 1,
        )
        backs.append(swap(back))
        done = back

    def do_slopes(c):
        nonlocal done
        slope, *kept = slopes_back(
            follow(order, done), firsts[c], backs[c], w_second, w2_t, w3_big
        )
        slopes.append((slope, *kept))
        done = slope

    def do_second_grads(c):
        nonlocal done, sums
        _, *kept = slopes[c]
        sums = second_grads(
            follow(turns, done), firsts[c], *kept, backs[c], sums, c == n_chunks - 1
        )
        done = sums

    def do_first_grad(c):
        nonlocal done, part_one, grad_four
        last = c == n_chunks - 1
        part_one = first_grad(
            gathered[c], order, follow(turns, done), slopes[c][0], n_g, in_width, part_one, last
        )
        done = part_one

    one_state = {}

    def do_ring_one(c):
        if not ring:
            return
        if c == 0:
            one = part_one.reshape(4, 2, n_dev, spread, n_g, in_width)
            one_state["parts"] = [one[:, h] for h in range(2)]
            one_state["got"] = [ring_send(one[:, h], SIDES[h][0]) for h in range(2)]
            return
        got = follow(one_state["got"], done)
        one_state["own"] = []
        for h in range(2):
            mine, part = ring_half(one_state["parts"][h], got[h], SIDES[h][1])
            one_state["own"].append((mine + part.astype(F32)).astype(BF16))

    four = {}

    def do_ring_four(c):
        nonlocal done, grad_four
        if not ring:
            return
        near, far = SIDES[0]
        rank = me_tok ^ jnp.arange(4)
        if c == 0:
            four["shape"] = grad_four.shape
            parts = jnp.take(grad_four.reshape(4, -1, LANES), rank, axis=0)
            four["parts"], four["got"] = parts, ring_send(parts, near)
        elif c == 1:
            got = follow(four["got"], done)
            four["mine"], four["got"] = ring_half(four["parts"], got, far)
            done = (done, four["mine"])
        elif c == 2:
            got = follow(four["got"], done)
            four["own"] = (four["mine"] + got.astype(F32)).astype(BF16)
            four["other"] = turn(four["own"], "tok", far)
            done = (done, four["own"])
        elif c == 3:
            pair = jnp.stack([four["own"], follow(four["other"], done)])
            four["pair"], four["got"] = pair, turn(pair, "tok", near)
            done = (done, pair)
        else:
            pair, got = four["pair"], follow(four["got"], done)
            parts = {0: pair[0], far: pair[1], near: got[0], 2: got[1]}
            parts = jnp.stack([parts[k] for k in range(4)])
            grad_four = jnp.take(parts, rank, axis=0).reshape(four["shape"]).astype(F32)

    steps = {
        "g": do_gather,
        "h": do_last_pieces,
        "q": do_ring_four,
        "r": do_ring_one,
        "f": do_forward,
        "m": do_middle,
        "s": do_slopes,
        "d": do_second_grads,
        "x": do_first_grad,
    }
    for step in PLAN:
        steps[step[0]](int(step[1]))
    rest = sums[0]
    if not ring:
        grad_four, rest = lax.psum((grad_four.astype(BF16), rest.astype(BF16)), "tok")
        grad_two, grad_three = rest[:, :fan].astype(F32), rest[:, fan:].astype(F32)
        part_one = part_one.transpose(1, 0, 2, 3, 4)
        part_one = part_one.reshape(n_dev, first_local, spread, n_g, in_width).astype(BF16)
        grad_one = unpack_first(lax.psum(swap(part_one), "tok"), spread)
        return (grad_one, grad_two, grad_three.transpose(0, 2, 1), grad_four.astype(F32))

    me = me_tok.reshape(1)
    own = swap(jnp.stack(one_state["own"], axis=1))
    rest = rest.reshape(4, 2, n_g // 8, *rest.shape[1:])
    rest_halves = []
    for h in range(2):
        mine = ring_scatter(rest[:, h], *SIDES[h]).astype(BF16)
        rest_halves.append(ring_gather(mine, *SIDES[h]))
    grad_two, grad_three = unpack_ring_rest(rest_halves, me, fan)
    one_halves = [ring_gather(own[:, h], *SIDES[h]) for h in range(2)]
    grad_one = unpack_ring_first(one_halves, me, spread)
    return (grad_one, grad_two, grad_three.transpose(0, 2, 1), grad_four)


def solution(mesh):
    placed = (
        P("tok", "blk"),
        P("tok", "blk"),
        P("blk", None, None),
        P("blk", None, None),
        P("blk", None, None),
        P("blk", None, None),
    )
    return jax.shard_map(
        functools.partial(shards, CUTS),
        mesh=mesh,
        in_specs=placed,
        out_specs=(
            P("blk", None, None),
            P("blk", None, None),
            P("blk", None, None),
            P("blk", None, None),
        ),
        check_vma=False,
    )
```
